32 devices in a mesh: seq: 8 (over z, core), head: 4 (over y, x).
Axes of the slice: x: 2, y: 2, z: 4, core: 2. Of those that a mesh axis runs over, the one named last changes fastest.
Arguments:
- queries: bfloat16 [2048, 8192], P('seq', 'head'), may hold values from -6 to 6
- key_input: bfloat16 [2048, 8192], P('seq', 'head'), may hold values from -6 to 6
- value_input: bfloat16 [2048, 8192], P('seq', 'head'), may hold values from -6 to 6
- out_gate: bfloat16 [2048, 8192], P('seq', 'head'), may hold values from -8 to 8
- log_decay: float32 [64, 2048], P('head', 'seq'), may hold values from -1 to 0, as said below
- norm_gain: float32 [8192], P('head'), may hold values from 0.1 to 1.9
- features: bfloat16 [2048, 6144], P('seq', 'head'), may hold values from -6 to 6
- expert_ids: int32 [2048, 2], P('seq'), may hold values from 0 to 31, as said below
- route_weight: float32 [2048, 2], P('seq'), may hold values from 0.25 to 1
- placement: int32 [4], replicated, may hold values from 0 to 31, as said below
- gate_weight: bfloat16 [6144, 36864], P('head', 'seq'), may hold values from -0.078125 to 0.078125
- up_weight: bfloat16 [6144, 36864], P('head', 'seq'), may hold values from -0.078125 to 0.078125
- down_weight: bfloat16 [36864, 6144], P('seq', 'head'), may hold values from -0.0625 to 0.0625
Outputs:
- attention_out: bfloat16 [2048, 8192], P('seq', 'head')
- moe_out: bfloat16 [2048, 6144], P('seq', 'head')
The draws below stay inside these ranges and needn't reach their ends.
Inputs may be any that keep to these rules, and one draw needn't show every extreme that they name: `expert_ids`: in each aligned block of 256 tokens, each expert named in placement is named by at most 8 tokens, and the same one of them by exactly 8 tokens in every block; the two ids of a token differ. `placement`: 4 different expert numbers, among them always 0 and 31. `log_decay`: every entry is negative.
All inputs are finite; a program needn't handle non-finite values.
Results may differ from the reference program's by a relative error of at most 0.0058.
Values may be sent and summed in bfloat16 or wider, within the bound.
A program may use at most 128 MiB of HBM per device.

```python
import jax
import jax.numpy as jnp
from jax import lax

D = 6144
HEADS = 64
HEAD_DIM = 128
FF = 9216
EXPERTS = 32
EXP_FLY = 4
TOK_DEV = 256
CAP = 8
SEQUENCE_TOKENS = 2048
N_SEQ = 8


def draw_log_decay(key, part):
    random_keys = jax.random.split(jax.random.fold_in(key, 11), 6)
    blocks = SEQUENCE_TOKENS // TOK_DEV
    fast_share = 0.5
    fast = jax.random.uniform(random_keys[0], (HEADS, 1), jnp.float32) < fast_share
    fast_rate = jnp.exp(jax.random.uniform(random_keys[1], (HEADS, 1), jnp.float32, jnp.log(1.0 / 50.0), jnp.log(1.0 / 30.0)))
    slow_rate = 0.25 / SEQUENCE_TOKENS * jnp.ones((HEADS, 1), jnp.float32)
    decay_rate = jnp.where(fast, fast_rate, slow_rate)
    block_decay_factor = jax.random.uniform(random_keys[2], (HEADS, blocks, 1), jnp.float32, 1.0, 2.0)
    block_decay_factor = jnp.broadcast_to(block_decay_factor, (HEADS, blocks, TOK_DEV)).reshape(HEADS, SEQUENCE_TOKENS)
    token_decay_factor = jnp.exp(jax.random.uniform(random_keys[3], (HEADS, SEQUENCE_TOKENS), jnp.float32, jnp.log(0.5), jnp.log(2.0)))
    spike_locations = jax.random.randint(random_keys[4], (3,), 0, SEQUENCE_TOKENS)
    spike_depth = jnp.log(jax.random.uniform(random_keys[5], (3,), jnp.float32, 0.5, 0.8))
    token_positions = jnp.arange(SEQUENCE_TOKENS)
    decay_spikes = jnp.sum(jnp.where(token_positions[None, :] == spike_locations[:, None], spike_depth[:, None], 0.0), axis=0)
    return -decay_rate * block_decay_factor * token_decay_factor + decay_spikes[None, :]


def route_plan(key):
    plan_keys = jax.random.split(jax.random.fold_in(key, 5), 2)
    middle = (jax.random.permutation(plan_keys[0], EXPERTS - 2) + 1)[:EXP_FLY - 2].astype(jnp.int32)
    ends = jnp.array([0, EXPERTS - 1], dtype=jnp.int32)
    chosen = jnp.concatenate([ends, middle], axis=0)
    order = jax.random.permutation(plan_keys[1], EXP_FLY)
    return chosen[order].astype(jnp.int32)


def draw_placement(key, part):
    return route_plan(key)


def draw_expert_ids(key, part):
    placement = route_plan(key)
    blocks = SEQUENCE_TOKENS // TOK_DEV
    random_keys = jax.random.split(jax.random.fold_in(key, 9), 4)
    full_slot = jax.random.randint(random_keys[0], (), 0, EXP_FLY)
    loads = jax.random.randint(random_keys[1], (blocks, EXP_FLY), CAP // 4, CAP + 1)
    loads = jnp.where(jnp.arange(EXP_FLY)[None, :] == full_slot, CAP, loads)
    rest = 2 * TOK_DEV - jnp.sum(loads, axis=1)
    others = EXPERTS - EXP_FLY
    base = rest // others
    extra = rest % others
    in_flight = (jnp.arange(EXPERTS)[:, None] == placement[None, :]).astype(jnp.int32)
    flying = jnp.sum(in_flight, axis=1)
    other_rank = jnp.cumsum(1 - flying) - 1
    counts_other = base[:, None] + (other_rank[None, :] < extra[:, None]).astype(jnp.int32)
    counts_fly = jnp.sum(in_flight[None, :, :] * loads[:, None, :], axis=2)
    counts = jnp.where(flying[None, :] == 1, counts_fly, counts_other)
    ends = jnp.cumsum(counts, axis=1)
    position = jnp.arange(2 * TOK_DEV)
    listed = jnp.sum((position[None, :, None] >= ends[:, None, :]).astype(jnp.int32), axis=2)
    pairs = jnp.stack([listed[:, :TOK_DEV], listed[:, TOK_DEV:]], axis=-1)
    orders = jax.vmap(lambda sub: jax.random.permutation(sub, TOK_DEV))(jax.random.split(random_keys[2], blocks))
    pairs = jnp.take_along_axis(pairs, orders[:, :, None], axis=1)
    flip = jax.random.randint(random_keys[3], (blocks, TOK_DEV, 1), 0, 2)
    pairs = jnp.where(flip == 1, pairs[:, :, ::-1], pairs)
    return pairs.reshape(SEQUENCE_TOKENS, 2).astype(jnp.int32)


def steps_of(key, shape, cuts, low, high):
    factor_of, own = 1.0, jax.random.fold_in(key, 6)
    for axis_at, parts in cuts:
        draws = jnp.exp(jax.random.uniform(jax.random.fold_in(own, axis_at), (parts,), jnp.float32, low / len(cuts), high / len(cuts)))
        factor_of = factor_of * jnp.repeat(draws, shape[axis_at] // parts).reshape([-1 if axis == axis_at else 1 for axis in range(len(shape))])
    return factor_of


def scatter_about(own_key, shape, scale, reach, cuts=(), kind=jnp.bfloat16):
    entries = scale * jax.random.normal(own_key, shape, jnp.float32)
    if cuts:
        entries = entries * steps_of(own_key, shape, cuts, -0.22, 0.18)
    return jnp.clip(entries, -reach, reach).astype(kind)


def setup_inputs(seed: int = 0) -> dict:
    seeds = jax.random.split(jax.random.key(seed), 14)
    queries = scatter_about(seeds[0], (SEQUENCE_TOKENS, HEADS * HEAD_DIM), 1.0, 6.0, ((0, 8), (1, 4)))
    key_input = scatter_about(seeds[1], (SEQUENCE_TOKENS, HEADS * HEAD_DIM), 1.0, 6.0, ((0, 8), (1, 4)))
    value_input = scatter_about(seeds[2], (SEQUENCE_TOKENS, HEADS * HEAD_DIM), 1.0, 6.0, ((0, 8), (1, 4)))
    out_gate = scatter_about(seeds[3], (SEQUENCE_TOKENS, HEADS * HEAD_DIM), 2.0, 8.0, ((0, 8), (1, 4)))
    log_decay = draw_log_decay(jax.random.fold_in(seeds[13], 71), 0)
    norm_gain = jnp.clip(1.0 + 0.18 * jax.random.normal(seeds[5], (HEADS * HEAD_DIM,), jnp.float32), 0.1, 1.9)
    features = scatter_about(seeds[6], (SEQUENCE_TOKENS, D), 1.0, 6.0, ((0, 8), (1, 4)))
    expert_ids = draw_expert_ids(jax.random.fold_in(seeds[13], 71), 0)
    route_weight = jnp.clip(0.25 + 0.75 * jax.random.uniform(seeds[8], (SEQUENCE_TOKENS, 2), jnp.float32) ** steps_of(seeds[8], (SEQUENCE_TOKENS, 2), ((0, 8),), -0.2, 0.2), 0.25, 1.0)
    placement = draw_placement(jax.random.fold_in(seeds[13], 71), 0)
    gate_weight = scatter_about(seeds[10], (D, EXP_FLY * FF), D ** -0.5, 0.078125, ((0, 4), (1, 8)))
    up_weight = scatter_about(seeds[11], (D, EXP_FLY * FF), D ** -0.5, 0.078125, ((0, 4), (1, 8)))
    down_weight = scatter_about(seeds[12], (EXP_FLY * FF, D), FF ** -0.5, 0.0625, ((0, 8), (1, 4)))
    return {"queries": queries, "key_input": key_input, "value_input": value_input, "out_gate": out_gate, "log_decay": log_decay, "norm_gain": norm_gain, "features": features, "expert_ids": expert_ids, "route_weight": route_weight, "placement": placement, "gate_weight": gate_weight, "up_weight": up_weight, "down_weight": down_weight}


def slot_table(pairs, placement):
    flat = pairs.reshape(-1)
    match = (flat[:, None] == placement[None, :]).astype(jnp.int32)
    rank = jnp.cumsum(match, axis=0) - 1
    order = jnp.arange(CAP, dtype=jnp.int32)
    hits = (match[None, :, :] == 1) & (rank[None, :, :] == order[:, None, None])
    return jnp.transpose(hits, (2, 0, 1))

def attention_part(queries, key_input, value_input, out_gate, log_decay, norm_gain):
    blocks = queries.shape[0] // TOK_DEV
    shape = (blocks, TOK_DEV, HEADS, HEAD_DIM)
    query_b = queries.reshape(shape)
    key_b = key_input.reshape(shape)
    value_b = value_input.reshape(shape)
    decay_b = jnp.transpose(log_decay.reshape(HEADS, blocks, TOK_DEV), (1, 0, 2))
    lower = jnp.arange(TOK_DEV)[:, None] >= jnp.arange(TOK_DEV)[None, :]

    def step(state, item):
        query_c, key_c, value_c, decay_c = item
        query_f = query_c.astype(jnp.float32)
        key_f = key_c.astype(jnp.float32)
        value_f = value_c.astype(jnp.float32)
        cum = jnp.cumsum(decay_c, axis=1)
        scores = jnp.einsum('thd,shd->hts', query_f, key_f)
        spread = cum[:, :, None] - cum[:, None, :]
        weights = jnp.exp(jnp.where(lower[None], spread, -jnp.inf))
        probs = lax.optimization_barrier((scores * weights).astype(jnp.bfloat16)).astype(jnp.float32)
        intra = jnp.einsum('hts,shd->thd', probs, value_f)
        query_s = query_f * jnp.exp(cum).T[:, :, None]
        inter = jnp.einsum('thd,hde->the', query_s, state, precision=lax.Precision.HIGHEST)
        last = cum[:, -1]
        key_s = key_f * jnp.exp(last[:, None] - cum).T[:, :, None]
        local = jnp.einsum('thd,the->hde', key_s, value_f, precision=lax.Precision.HIGHEST)
        new_state = jnp.exp(last)[:, None, None] * state + local
        return (new_state, intra + inter)
    start = jnp.zeros((HEADS, HEAD_DIM, HEAD_DIM), jnp.float32)
    _, mixed = lax.scan(step, start, (query_b, key_b, value_b, decay_b))
    mixed = mixed.reshape(-1, HEADS, HEAD_DIM)
    power = lax.optimization_barrier(jnp.mean(mixed * mixed, axis=-1, keepdims=True))
    normed = mixed * lax.rsqrt(power + 1e-06)
    gates = jax.nn.sigmoid(out_gate.reshape(-1, HEADS, HEAD_DIM).astype(jnp.float32))
    result = normed * norm_gain.reshape(HEADS, HEAD_DIM) * gates
    return result.reshape(-1, HEADS * HEAD_DIM).astype(jnp.bfloat16)

def experts_part(features, expert_ids, route_weight, placement, gate_weight, up_weight, down_weight):
    blocks = features.shape[0] // TOK_DEV
    group = N_SEQ // EXP_FLY
    slice_width = FF // group
    hits = jax.vmap(lambda pairs: slot_table(pairs, placement))(expert_ids.reshape(blocks, TOK_DEV, 2))
    hits = hits.reshape(blocks, EXP_FLY, CAP, TOK_DEV, 2).astype(jnp.float32)
    pick = lax.optimization_barrier(jnp.sum(hits, axis=4))
    share = lax.optimization_barrier(jnp.sum(hits * route_weight.reshape(blocks, 1, 1, TOK_DEV, 2), axis=4))
    feats = features.reshape(blocks, TOK_DEV, D).astype(jnp.float32)
    rows = jnp.einsum('bjct,btd->jbcd', pick, feats).astype(jnp.bfloat16)

    def one_expert(item):
        chosen, index = item
        chosen = chosen.reshape(blocks * CAP, D)
        start = index * FF
        gate_cols = lax.dynamic_slice_in_dim(gate_weight, start, FF, 1)
        up_cols = lax.dynamic_slice_in_dim(up_weight, start, FF, 1)
        down_rows = lax.dynamic_slice_in_dim(down_weight, start, FF, 0)
        gate = jnp.dot(chosen, gate_cols, preferred_element_type=jnp.float32)
        up = jnp.dot(chosen, up_cols, preferred_element_type=jnp.float32)
        hidden = lax.optimization_barrier((jax.nn.silu(gate) * up).astype(jnp.bfloat16))
        hidden = hidden.astype(jnp.float32).reshape(-1, group, slice_width)
        pieces = jnp.einsum('rgf,gfd->rgd', hidden, down_rows.astype(jnp.float32).reshape(group, slice_width, D))
        pieces = lax.optimization_barrier(pieces.astype(jnp.bfloat16)).astype(jnp.float32)
        return lax.optimization_barrier(jnp.sum(pieces, axis=1)).reshape(blocks, CAP, D)
    outs = lax.map(one_expert, (rows, jnp.arange(EXP_FLY, dtype=jnp.int32)))
    mixed = jnp.einsum('bjct,jbcd->btd', share, outs, precision=lax.Precision.HIGHEST)
    return mixed.reshape(-1, D).astype(jnp.bfloat16)

def reference(queries, key_input, value_input, out_gate, log_decay, norm_gain, features, expert_ids, route_weight, placement, gate_weight, up_weight, down_weight):
    attention_out = attention_part(queries, key_input, value_input, out_gate, log_decay, norm_gain)
    moe_out = experts_part(features, expert_ids, route_weight, placement, gate_weight, up_weight, down_weight)
    return (attention_out, moe_out)
```

```python
import functools

import jax
import jax.numpy as jnp
from jax import lax
from jax.experimental import pallas as pl
from jax.experimental.pallas import tpu as pltpu
from jax.sharding import PartitionSpec as P

CAP = 8
norm_eps = 1e-06
SLOTS = 4
F32, BF16 = jnp.float32, jnp.bfloat16


def each(count, body):
    if count <= 8:
        for i in range(count):
            body(i)
    else:

        @pl.loop(0, count)
        def _(i):
            body(i)


def dot(a, b, ca=1, cb=0):
    return lax.dot_general(a, b, (((ca,), (cb,)), ((), ())), preferred_element_type=F32)


def kernel(
    cfg,
    ld, gain, ids, rw, place,
    q_hbm, k_hbm, v_hbm, g_hbm, f_hbm, wg_hbm, wu_hbm, wd_hbm,
    ao_hbm, mo_hbm,
    q, k, v, g, f, wg, wu, wd, ao, mo,
    cum, cum_t, carry, carry_in, loc, loc_in, s_in, s_out, st, intra,
    share, out_x, in_x, x, rs_out, rs_in, hid, acc, out_y, in_y,
    local_sem, weight_sem, x_send, x_recv, rs_send, rs_recv, ag_send, ag_recv,
    y_send, y_recv, chain_sem, out_sem,
):
    n_seq, n_head, experts, chunks, width, heads, hd, half = cfg
    tokens = q.shape[0]
    depth = f.shape[1]
    group = n_seq // experts
    rows = n_seq * CAP
    per = rows // n_head
    seq, head = lax.axis_index("seq"), lax.axis_index("head")
    core, chip, chips = lax.rem(seq, 2), seq // 2, n_seq // 2

    def at_seq(i):
        return {"seq": i}

    def at_head(i):
        return {"head": i}

    barrier = pltpu.get_barrier_semaphore()

    def greet_seq(r):
        pl.semaphore_signal(barrier, inc=1, device_id=at_seq(lax.rem(seq + r + 1, n_seq)),
                            device_id_type=pl.DeviceIdType.MESH)

    def greet_head(r):
        pl.semaphore_signal(barrier, inc=1, device_id=at_head(lax.rem(head + r + 1, n_head)),
                            device_id_type=pl.DeviceIdType.MESH)

    each(n_seq - 1, greet_seq)
    each(n_head - 1, greet_head)

    local = [
        pltpu.make_async_copy(a, b, local_sem.at[i])
        for i, (a, b) in enumerate(((f_hbm, f), (k_hbm, k), (v_hbm, v), (q_hbm, q), (g_hbm, g)))
    ]
    for copy in local[:3]:
        copy.start()
    up_copies, down_copies = [], []
    for c in range(chunks):
        cols = pl.ds(c * width, width)
        up_copies.append((
            pltpu.make_async_copy(wg_hbm.at[:, cols], wg.at[c], weight_sem.at[0, c]),
            pltpu.make_async_copy(wu_hbm.at[:, cols], wu.at[c], weight_sem.at[1, c]),
        ))
        down_copies.append(pltpu.make_async_copy(wd_hbm.at[cols, :], wd.at[c], weight_sem.at[2, c]))
    for a, b in up_copies:
        a.start()
        b.start()
    for copy in local[3:]:
        copy.start()
    for copy in down_copies:
        copy.start()

    t_row = lax.broadcasted_iota(jnp.int32, (tokens, tokens), 0)
    t_col = lax.broadcasted_iota(jnp.int32, (tokens, tokens), 1)
    lower = (t_row >= t_col).astype(F32).astype(BF16)
    slots = experts * CAP
    lane = lax.broadcasted_iota(jnp.int32, (tokens, slots), 1)
    wanted = jnp.full((tokens, slots), -1, jnp.int32)
    for j in range(experts):
        wanted = jnp.where(lane // CAP == j, place[j], wanted)
    first = (ids[:, 0:1] == wanted).astype(F32)
    second = (ids[:, 1:2] == wanted).astype(F32)
    match = first + second
    rank = dot(lower, match.astype(BF16))
    hit = jnp.where(rank == (lane % CAP + 1).astype(F32), match, 0.0)
    share[...] = hit * (first * rw[:, 0:1] + second * rw[:, 1:2])
    local[0].wait()
    picked = dot(hit.astype(BF16), f[...], 0, 0)
    pad = 2 * half - depth

    def pack(a):
        high = a[:, half:]
        if pad:
            high = jnp.concatenate([high, jnp.zeros((CAP, pad), F32)], axis=1)
        return jnp.concatenate([a[:, :half], high], axis=0).astype(BF16)

    for j in range(experts):
        out_x[j] = pack(picked[j * CAP:(j + 1) * CAP])
    in_x[seq] = out_x[seq // group]
    pl.semaphore_wait(barrier, n_seq - 1 + n_head - 1)

    def x_copy(r):
        to = lax.rem(seq + r + 1, n_seq)
        return pltpu.make_async_remote_copy(
            out_x.at[to // group], in_x.at[seq], x_send.at[r], x_recv.at[r],
            device_id=at_seq(to), device_id_type=pl.DeviceIdType.MESH)

    def x_arrival(r):
        src = lax.rem(seq + n_seq - r - 1, n_seq)
        return pltpu.make_async_remote_copy(
            out_x.at[0], in_x.at[src], x_send.at[r], x_recv.at[r],
            device_id=at_seq(src), device_id_type=pl.DeviceIdType.MESH)

    each(n_seq - 1, lambda r: x_copy(r).start())

    rest = ld[...]
    total, total_t = 0.0, 0.0
    for _ in range(3):
        piece = rest.astype(BF16)
        rest = rest - piece.astype(F32)
        total = total + dot(piece, lower, 1, 1)
        total_t = total_t + dot(lower, piece, 1, 1)
    cum[...] = total
    cum_t[...] = total_t
    carry[...] = jnp.broadcast_to(jnp.exp(total[:, tokens - 1:]), carry.shape)
    head_lane = lax.broadcasted_iota(jnp.int32, (tokens, heads), 1)

    def column(h):
        return jnp.sum(jnp.where(head_lane == h, cum_t[...], 0.0), axis=1, keepdims=True)

    def cols_of(h):
        return pl.ds(pl.multiple_of(h * hd, hd), hd)

    local[1].wait()
    local[2].wait()

    def own_state(h, _):
        col = column(h)
        scaled = k[:, cols_of(h)].astype(F32) * jnp.exp(col[tokens - 1:] - col)
        loc[h] = dot(scaled.astype(BF16), v[:, cols_of(h)], 0, 0).astype(BF16)
        return 0

    lax.fori_loop(0, heads, own_state, 0, unroll=True)

    def pair_copy(ref, to, n, other):
        return pltpu.make_async_remote_copy(
            ref, to, chain_sem.at[0, n], chain_sem.at[1, n],
            device_id=at_seq(other), device_id_type=pl.DeviceIdType.MESH)

    partner = seq + 1 - 2 * core
    onward = lax.rem(seq + 2, n_seq)
    loc_copy = pair_copy(loc, loc_in, 0, partner)
    carry_copy = pair_copy(carry, carry_in, 1, partner)
    state_copy = pair_copy(s_out, s_in, 2, onward)
    share_copy = pair_copy(s_in, st, 3, partner)

    @pl.when(core == 0)
    def _():
        loc_copy.start()
        carry_copy.start()

    def chain(which):
        @pl.when((core == 1) & which)
        def _():
            loc_copy.wait_recv()
            carry_copy.wait_recv()

            @pl.when(chip == 0)
            def _():
                s_in[...] = jnp.zeros_like(s_in)

            @pl.when(chip > 0)
            def _():
                state_copy.wait_recv()

            share_copy.start()

            def step(h, _):
                mid = carry_in[pl.ds(h, 1)] * s_in[h].astype(F32) + loc_in[h].astype(F32)
                st[h] = mid.astype(BF16)
                s_out[h] = (carry[pl.ds(h, 1)] * mid + loc[h].astype(F32)).astype(BF16)
                return 0

            lax.fori_loop(0, heads, step, 0)

            @pl.when(chip < chips - 1)
            def _():
                state_copy.start()

    each(n_seq - 1, lambda r: x_arrival(r).wait_recv())
    both = in_x[...].astype(F32)
    low = both[:, :CAP].reshape(rows, half)
    high = both[:, CAP:].reshape(rows, half)[:, :depth - half]
    x[...] = jnp.concatenate([low, high], axis=1).astype(BF16)
    chain(chip == 0)

    def rs_copy(c, r):
        to = lax.rem(head + r + 1, n_head)
        return pltpu.make_async_remote_copy(
            rs_out.at[c, to], rs_in.at[c, r], rs_send.at[c, r], rs_recv.at[c, r],
            device_id=at_head(to), device_id_type=pl.DeviceIdType.MESH)

    def ag_copy(c, r, src):
        to = lax.rem(head + r + 1, n_head)
        return pltpu.make_async_remote_copy(
            hid.at[c, src], hid.at[c, src], ag_send.at[c, r], ag_recv.at[c, r],
            device_id=at_head(to), device_id_type=pl.DeviceIdType.MESH)

    for c in range(chunks):
        for which, ref in enumerate((wg, wu)):
            up_copies[c][which].wait()
            part = dot(x[...], ref[c])
            rs_out[c, :, which] = part.astype(BF16).reshape(n_head, per, width)
        each(n_head - 1, lambda r, c=c: rs_copy(c, r).start())
    chain(chip == 1)

    def within(h, _):
        qh, kh, vh = (a[:, cols_of(h)] for a in (q, k, v))
        spread = column(h) - cum[pl.ds(h, 1)]
        decay = jnp.exp(jnp.where(t_row >= t_col, spread, -jnp.inf))
        probs = (dot(qh, kh, 1, 1) * decay).astype(BF16)
        intra[:, cols_of(h)] = dot(probs, vh)
        return 0

    local[3].wait()
    parts = min(chunks, heads)
    bounds = [heads * i // parts for i in range(parts + 1)]
    for c in range(chunks):
        if c < parts:
            lax.fori_loop(bounds[c], bounds[c + 1], within, 0, unroll=True)
        each(n_head - 1, lambda r, c=c: rs_copy(c, r).wait_recv())
        gate = rs_out[c, head, 0].astype(F32)
        up = rs_out[c, head, 1].astype(F32)
        for r in range(n_head - 1):
            gate += rs_in[c, r, 0].astype(F32)
            up += rs_in[c, r, 1].astype(F32)
        hid[c, head] = (gate / (1.0 + jnp.exp(-gate)) * up).astype(BF16)
        each(n_head - 1, lambda r, c=c: ag_copy(c, r, head).start())
    chain(chip == 2)

    for c in range(chunks):
        each(n_head - 1, lambda r, c=c: ag_copy(c, r, lax.rem(head + n_head - r - 1, n_head)).wait_recv())
        down_copies[c].wait()
        part = dot(hid[c].reshape(rows, width), wd[c])
        if c == 0:
            acc[...] = part
        else:
            acc[...] += part

    for b in range(n_seq):
        out_y[b] = pack(acc[b * CAP:(b + 1) * CAP, :])
    in_y[seq] = out_y[seq]

    def y_copy(r):
        to = lax.rem(seq + r + 1, n_seq)
        return pltpu.make_async_remote_copy(
            out_y.at[to], in_y.at[seq], y_send.at[r], y_recv.at[r],
            device_id=at_seq(to), device_id_type=pl.DeviceIdType.MESH)

    def y_arrival(r):
        src = lax.rem(seq + n_seq - r - 1, n_seq)
        return pltpu.make_async_remote_copy(
            out_y.at[0], in_y.at[src], y_send.at[r], y_recv.at[r],
            device_id=at_seq(src), device_id_type=pl.DeviceIdType.MESH)

    each(n_seq - 1, lambda r: y_copy(r).start())
    chain(chip >= SLOTS - 1)

    @pl.when(core == 0)
    def _():
        share_copy.wait_recv()

    local[4].wait()

    def finish(h, _):
        cols = cols_of(h)
        mixed = intra[:, cols] + jnp.exp(column(h)) * dot(q[:, cols], st[h])
        power = jnp.mean(mixed * mixed, axis=-1, keepdims=True)
        gates = 1.0 / (1.0 + jnp.exp(-g[:, cols].astype(F32)))
        ao[:, cols] = (mixed * lax.rsqrt(power + norm_eps) * gain[:, cols] * gates).astype(BF16)
        return 0

    lax.fori_loop(0, heads, finish, 0, unroll=True)
    ao_copy = pltpu.make_async_copy(ao, ao_hbm, out_sem.at[0])
    ao_copy.start()

    each(n_seq - 1, lambda r: y_arrival(r).wait_recv())
    outs = []
    for j in range(experts):
        both = in_y[j * group].astype(F32)
        for i in range(1, group):
            both += in_y[j * group + i].astype(F32)
        outs.append(jnp.concatenate([both[:CAP], both[CAP:, :depth - half]], axis=1))
    mo[...] = dot(share[...], jnp.concatenate(outs, axis=0)).astype(BF16)
    mo_copy = pltpu.make_async_copy(mo, mo_hbm, out_sem.at[1])
    mo_copy.start()

    each(n_seq - 1, lambda r: x_copy(r).wait_send())
    each(n_seq - 1, lambda r: y_copy(r).wait_send())
    for c in range(chunks):
        each(n_head - 1, lambda r, c=c: rs_copy(c, r).wait_send())
        each(n_head - 1, lambda r, c=c: ag_copy(c, r, head).wait_send())

    @pl.when(core == 0)
    def _():
        loc_copy.wait_send()
        carry_copy.wait_send()

    @pl.when(core == 1)
    def _():
        share_copy.wait_send()

        @pl.when(chip < chips - 1)
        def _():
            state_copy.wait_send()

    ao_copy.wait()
    mo_copy.wait()


def per_device(
    queries, key_input, value_input, out_gate, log_decay, norm_gain, features,
    expert_ids, route_weight, placement, gate_weight, up_weight, down_weight,
):
    n_seq, n_head = lax.axis_size("seq"), lax.axis_size("head")
    experts = placement.shape[0]
    tokens, inner = queries.shape
    heads = log_decay.shape[0]
    hd = inner // heads
    depth, hidden = gate_weight.shape
    half = -(-depth // 256) * 128
    chunks = next((n for n in (6, 4, 3, 2) if hidden % (n * 128) == 0), 1)
    width = hidden // chunks
    rows = n_seq * CAP
    per = rows // n_head
    cfg = (n_seq, n_head, experts, chunks, width, heads, hd, half)
    square = (heads, hd, hd)
    vm = pltpu.VMEM
    dma = pltpu.SemaphoreType.DMA
    vmem, anywhere = pl.BlockSpec(memory_space=pltpu.VMEM), pl.BlockSpec(memory_space=pl.ANY)
    scratch = [
        vm((tokens, inner), BF16), vm((tokens, inner), BF16), vm((tokens, inner), BF16),
        vm((tokens, inner), BF16), vm((tokens, depth), BF16),
        vm((chunks, depth, width), BF16), vm((chunks, depth, width), BF16),
        vm((chunks, width, depth), BF16), vm((tokens, inner), BF16), vm((tokens, depth), BF16),
        vm((heads, tokens), F32), vm((tokens, heads), F32), vm((heads, hd), F32), vm((heads, hd), F32),
        vm(square, BF16), vm(square, BF16), vm(square, BF16), vm(square, BF16), vm(square, BF16),
        vm((tokens, inner), F32),
        vm((tokens, experts * CAP), F32), vm((experts, 2 * CAP, half), BF16),
        vm((n_seq, 2 * CAP, half), BF16), vm((rows, depth), BF16),
        vm((chunks, n_head, 2, per, width), BF16), vm((chunks, n_head - 1, 2, per, width), BF16),
        vm((chunks, n_head, per, width), BF16), vm((rows, depth), F32),
        vm((n_seq, 2 * CAP, half), BF16), vm((n_seq, 2 * CAP, half), BF16),
        dma((5,)), dma((3, chunks)), dma((n_seq - 1,)), dma((n_seq - 1,)),
        dma((chunks, n_head - 1)), dma((chunks, n_head - 1)),
        dma((chunks, n_head - 1)), dma((chunks, n_head - 1)),
        dma((n_seq - 1,)), dma((n_seq - 1,)), dma((2, 4)), dma((2,)),
    ]
    return pl.pallas_call(
        functools.partial(kernel, cfg),
        out_shape=(
            jax.ShapeDtypeStruct((tokens, inner), BF16),
            jax.ShapeDtypeStruct((tokens, depth), BF16),
        ),
        in_specs=[vmem] * 4 + [pl.BlockSpec(memory_space=pltpu.SMEM)] + [anywhere] * 8,
        out_specs=(anywhere, anywhere),
        scratch_shapes=scratch,
        compiler_params=pltpu.CompilerParams(
            collective_id=0, has_side_effects=True, vmem_limit_bytes=60 * 1024 * 1024
        ),
    )(
        log_decay, norm_gain.reshape(1, -1), expert_ids, route_weight, placement,
        queries, key_input, value_input, out_gate, features, gate_weight, up_weight, down_weight,
    )


def solution(mesh):
    placed = (
        P("seq", "head"), P("seq", "head"), P("seq", "head"), P("seq", "head"),
        P("head", "seq"), P("head"), P("seq", "head"), P("seq", None), P("seq", None), P(),
        P("head", "seq"), P("head", "seq"), P("seq", "head"),
    )
    return jax.shard_map(
        per_device,
        mesh=mesh,
        in_specs=placed,
        out_specs=(P("seq", "head"), P("seq", "head")),
        check_vma=False,
    )
```

```python
import functools

import jax
import jax.numpy as jnp
from jax import lax
from jax.experimental import pallas as pl
from jax.experimental.pallas import tpu as pltpu
from jax.sharding import PartitionSpec as P

CAP = 8
norm_eps = 1e-06
SLOTS = 4
F32, BF16 = jnp.float32, jnp.bfloat16


def each(count, body):
    if count <= 8:
        for i in range(count):
            body(i)
    else:

        @pl.loop(0, count)
        def _(i):
            body(i)


def dot(a, b, ca=1, cb=0):
    return lax.dot_general(a, b, (((ca,), (cb,)), ((), ())), preferred_element_type=F32)


def kernel(
    cfg,
    ld, gain, ids, rw, place,
    q_hbm, k_hbm, v_hbm, g_hbm, f_hbm, wg_hbm, wu_hbm, wd_hbm,
    ao_hbm, mo_hbm,
    q, k, v, g, f, wg, wu, wd, ao, mo,
    cum, cum_t, carry, carry_in, loc, loc_in, s_in, s_out, st, intra,
    share, out_x, in_x, x, rs_out, rs_in, hid, acc, out_y, in_y,
    local_sem, weight_sem, x_send, x_recv, rs_send, rs_recv, ag_send, ag_recv,
    y_send, y_recv, chain_sem, out_sem,
):
    n_seq, n_head, experts, chunks, width, heads, hd, half = cfg
    tokens = q.shape[0]
    depth = f.shape[1]
    group = n_seq // experts
    rows = n_seq * CAP
    per = rows // n_head
    seq, head = lax.axis_index("seq"), lax.axis_index("head")
    core, chip, chips = lax.rem(seq, 2), seq // 2, n_seq // 2

    def at_seq(i):
        return {"seq": i}

    def at_head(i):
        return {"head": i}

    barrier = pltpu.get_barrier_semaphore()

    def greet_seq(r):
        pl.semaphore_signal(barrier, inc=1, device_id=at_seq(lax.rem(seq + r + 1, n_seq)),
                            device_id_type=pl.DeviceIdType.MESH)

    def greet_head(r):
        pl.semaphore_signal(barrier, inc=1, device_id=at_head(lax.rem(head + r + 1, n_head)),
                            device_id_type=pl.DeviceIdType.MESH)

    each(n_seq - 1, greet_seq)
    each(n_head - 1, greet_head)

    local = [
        pltpu.make_async_copy(a, b, local_sem.at[i])
        for i, (a, b) in enumerate(((f_hbm, f), (k_hbm, k), (v_hbm, v), (q_hbm, q), (g_hbm, g)))
    ]
    for copy in local[:3]:
        copy.start()
    up_copies, down_copies = [], []
    for c in range(chunks):
        cols = pl.ds(c * width, width)
        up_copies.append((
            pltpu.make_async_copy(wg_hbm.at[:, cols], wg.at[c], weight_sem.at[0, c]),
            pltpu.make_async_copy(wu_hbm.at[:, cols], wu.at[c], weight_sem.at[1, c]),
        ))
        down_copies.append(pltpu.make_async_copy(wd_hbm.at[cols, :], wd.at[c], weight_sem.at[2, c]))
    for a, b in up_copies:
        a.start()
        b.start()
    for copy in local[3:]:
        copy.start()
    for copy in down_copies:
        copy.start()

    t_row = lax.broadcasted_iota(jnp.int32, (tokens, tokens), 0)
    t_col = lax.broadcasted_iota(jnp.int32, (tokens, tokens), 1)
    lower = (t_row >= t_col).astype(F32).astype(BF16)
    slots = experts * CAP
    slot = lax.broadcasted_iota(jnp.int32, (slots, tokens), 0)
    wanted = jnp.full((slots, tokens), -1, jnp.int32)
    for j in range(experts):
        wanted = jnp.where(slot // CAP == j, place[j], wanted)
    first = (ids[0:1] == wanted).astype(F32)
    second = (ids[1:2] == wanted).astype(F32)
    match = first + second
    rank = dot(match.astype(BF16), lower, 1, 1)
    hit = jnp.where(rank == (slot % CAP + 1).astype(F32), match, 0.0)
    weight = hit * (first * rw[0:1] + second * rw[1:2])
    weight_high = weight.astype(BF16)
    share[0:slots] = weight_high.astype(F32)
    share[slots:] = weight - weight_high.astype(F32)
    local[0].wait()
    picked = dot(hit.astype(BF16), f[...])
    pad = 2 * half - depth

    def pack(a):
        high = a[:, half:]
        if pad:
            high = jnp.concatenate([high, jnp.zeros((CAP, pad), F32)], axis=1)
        return jnp.concatenate([a[:, :half], high], axis=0).astype(BF16)

    for j in range(experts):
        out_x[j] = pack(picked[j * CAP:(j + 1) * CAP])
    in_x[seq] = out_x[seq // group]
    pl.semaphore_wait(barrier, n_seq - 1 + n_head - 1)

    def x_copy(r):
        to = lax.rem(seq + r + 1, n_seq)
        return pltpu.make_async_remote_copy(
            out_x.at[to // group], in_x.at[seq], x_send.at[r], x_recv.at[r],
            device_id=at_seq(to), device_id_type=pl.DeviceIdType.MESH)

    def x_arrival(r):
        src = lax.rem(seq + n_seq - r - 1, n_seq)
        return pltpu.make_async_remote_copy(
            out_x.at[0], in_x.at[src], x_send.at[r], x_recv.at[r],
            device_id=at_seq(src), device_id_type=pl.DeviceIdType.MESH)

    each(n_seq - 1, lambda r: x_copy(r).start())

    rest = ld[...]
    total, total_t = 0.0, 0.0
    for _ in range(3):
        piece = rest.astype(BF16)
        rest = rest - piece.astype(F32)
        total = total + dot(piece, lower, 1, 1)
        total_t = total_t + dot(lower, piece, 1, 1)
    cum[...] = total
    cum_t[...] = total_t
    carry[...] = jnp.broadcast_to(jnp.exp(total[:, tokens - 1:]), carry.shape)
    head_lane = lax.broadcasted_iota(jnp.int32, (tokens, heads), 1)

    def column(h):
        return jnp.sum(jnp.where(head_lane == h, cum_t[...], 0.0), axis=1, keepdims=True)

    def cols_of(h):
        return pl.ds(pl.multiple_of(h * hd, hd), hd)

    local[1].wait()
    local[2].wait()

    def own_state(h, _):
        col = column(h)
        scaled = k[:, cols_of(h)].astype(F32) * jnp.exp(col[tokens - 1:] - col)
        loc[h] = dot(scaled.astype(BF16), v[:, cols_of(h)], 0, 0).astype(BF16)
        return 0

    lax.fori_loop(0, heads, own_state, 0, unroll=True)

    def pair_copy(ref, to, n, other):
        return pltpu.make_async_remote_copy(
            ref, to, chain_sem.at[0, n], chain_sem.at[1, n],
            device_id=at_seq(other), device_id_type=pl.DeviceIdType.MESH)

    partner = seq + 1 - 2 * core
    onward = lax.rem(seq + 2, n_seq)
    loc_copy = pair_copy(loc, loc_in, 0, partner)
    carry_copy = pair_copy(carry, carry_in, 1, partner)
    state_copy = pair_copy(s_out, s_in, 2, onward)
    share_copy = pair_copy(s_in, st, 3, partner)

    @pl.when(core == 0)
    def _():
        loc_copy.start()
        carry_copy.start()

    def chain(which):
        @pl.when((core == 1) & which)
        def _():
            loc_copy.wait_recv()
            carry_copy.wait_recv()

            @pl.when(chip == 0)
            def _():
                s_in[...] = jnp.zeros_like(s_in)

            @pl.when(chip > 0)
            def _():
                state_copy.wait_recv()

            share_copy.start()

            def step(h, _):
                mid = carry_in[pl.ds(h, 1)] * s_in[h].astype(F32) + loc_in[h].astype(F32)
                st[h] = mid.astype(BF16)
                s_out[h] = (carry[pl.ds(h, 1)] * mid + loc[h].astype(F32)).astype(BF16)
                return 0

            lax.fori_loop(0, heads, step, 0)

            @pl.when(chip < chips - 1)
            def _():
                state_copy.start()

    each(n_seq - 1, lambda r: x_arrival(r).wait_recv())
    both = in_x[...].astype(F32)
    low = both[:, :CAP].reshape(rows, half)
    high = both[:, CAP:].reshape(rows, half)[:, :depth - half]
    x[...] = jnp.concatenate([low, high], axis=1).astype(BF16)

    def rs_copy(c, r):
        to = lax.rem(head + r + 1, n_head)
        return pltpu.make_async_remote_copy(
            rs_out.at[c, to], rs_in.at[c, r], rs_send.at[c, r], rs_recv.at[c, r],
            device_id=at_head(to), device_id_type=pl.DeviceIdType.MESH)

    def ag_copy(c, r, src):
        to = lax.rem(head + r + 1, n_head)
        return pltpu.make_async_remote_copy(
            hid.at[c, src], hid.at[c, src], ag_send.at[c, r], ag_recv.at[c, r],
            device_id=at_head(to), device_id_type=pl.DeviceIdType.MESH)

    for c in range(chunks):
        for which, ref in enumerate((wg, wu)):
            up_copies[c][which].wait()
            part = dot(x[...], ref[c])
            rs_out[c, :, which] = part.astype(BF16).reshape(n_head, per, width)
        each(n_head - 1, lambda r, c=c: rs_copy(c, r).start())
        if c == 0:
            chain(chip == 0)

    def within(h, _):
        qh, kh, vh = (a[:, cols_of(h)] for a in (q, k, v))
        spread = column(h) - cum[pl.ds(h, 1)]
        decay = jnp.exp(jnp.where(t_row >= t_col, spread, -jnp.inf))
        probs = (dot(qh, kh, 1, 1) * decay).astype(BF16)
        intra[:, cols_of(h)] = dot(probs, vh)
        return 0

    local[3].wait()
    parts = min(chunks, heads)
    bounds = [heads * i // parts for i in range(parts + 1)]
    for c in range(chunks):
        if c < parts:
            lax.fori_loop(bounds[c], bounds[c + 1], within, 0, unroll=True)
        each(n_head - 1, lambda r, c=c: rs_copy(c, r).wait_recv())
        gate = rs_out[c, head, 0].astype(F32)
        up = rs_out[c, head, 1].astype(F32)
        for r in range(n_head - 1):
            gate += rs_in[c, r, 0].astype(F32)
            up += rs_in[c, r, 1].astype(F32)
        hid[c, head] = (gate / (1.0 + jnp.exp(-gate)) * up).astype(BF16)
        each(n_head - 1, lambda r, c=c: ag_copy(c, r, head).start())
        if c == 0:
            chain(chip == 1)
        if c == chunks - 1:
            chain(chip == 2)

    for c in range(chunks):
        each(n_head - 1, lambda r, c=c: ag_copy(c, r, lax.rem(head + n_head - r - 1, n_head)).wait_recv())
        down_copies[c].wait()
        part = dot(hid[c].reshape(rows, width), wd[c])
        if c == 0:
            acc[...] = part
        else:
            acc[...] += part

    for b in range(n_seq):
        out_y[b] = pack(acc[b * CAP:(b + 1) * CAP, :])
    in_y[seq] = out_y[seq]

    def y_copy(r):
        to = lax.rem(seq + r + 1, n_seq)
        return pltpu.make_async_remote_copy(
            out_y.at[to], in_y.at[seq], y_send.at[r], y_recv.at[r],
            device_id=at_seq(to), device_id_type=pl.DeviceIdType.MESH)

    def y_arrival(r):
        src = lax.rem(seq + n_seq - r - 1, n_seq)
        return pltpu.make_async_remote_copy(
            out_y.at[0], in_y.at[src], y_send.at[r], y_recv.at[r],
            device_id=at_seq(src), device_id_type=pl.DeviceIdType.MESH)

    each(n_seq - 1, lambda r: y_copy(r).start())
    chain(chip >= SLOTS - 1)

    @pl.when(core == 0)
    def _():
        share_copy.wait_recv()

    local[4].wait()

    def finish(h, _):
        cols = cols_of(h)
        mixed = intra[:, cols] + jnp.exp(column(h)) * dot(q[:, cols], st[h])
        power = jnp.mean(mixed * mixed, axis=-1, keepdims=True)
        gates = 1.0 / (1.0 + jnp.exp(-g[:, cols].astype(F32)))
        ao[:, cols] = (mixed * lax.rsqrt(power + norm_eps) * gain[:, cols] * gates).astype(BF16)
        return 0

    lax.fori_loop(0, heads, finish, 0, unroll=True)
    ao_copy = pltpu.make_async_copy(ao, ao_hbm, out_sem.at[0])
    ao_copy.start()

    each(n_seq - 1, lambda r: y_arrival(r).wait_recv())
    terms = []
    for i in range(group):
        outs = []
        for j in range(experts):
            both = in_y[j * group + i].astype(F32)
            outs.append(jnp.concatenate([both[:CAP], both[CAP:, :depth - half]], axis=1))
        terms += [jnp.concatenate(outs, axis=0).astype(BF16)] * 2
    weights = jnp.concatenate([share[...].astype(BF16)] * group, axis=0)
    mo[...] = dot(weights, jnp.concatenate(terms, axis=0), 0, 0).astype(BF16)
    mo_copy = pltpu.make_async_copy(mo, mo_hbm, out_sem.at[1])
    mo_copy.start()

    each(n_seq - 1, lambda r: x_copy(r).wait_send())
    each(n_seq - 1, lambda r: y_copy(r).wait_send())
    for c in range(chunks):
        each(n_head - 1, lambda r, c=c: rs_copy(c, r).wait_send())
        each(n_head - 1, lambda r, c=c: ag_copy(c, r, head).wait_send())

    @pl.when(core == 0)
    def _():
        loc_copy.wait_send()
        carry_copy.wait_send()

    @pl.when(core == 1)
    def _():
        share_copy.wait_send()

        @pl.when(chip < chips - 1)
        def _():
            state_copy.wait_send()

    ao_copy.wait()
    mo_copy.wait()


def per_device(
    queries, key_input, value_input, out_gate, log_decay, norm_gain, features,
    expert_ids, route_weight, placement, gate_weight, up_weight, down_weight,
):
    n_seq, n_head = lax.axis_size("seq"), lax.axis_size("head")
    experts = placement.shape[0]
    tokens, inner = queries.shape
    heads = log_decay.shape[0]
    hd = inner // heads
    depth, hidden = gate_weight.shape
    half = -(-depth // 256) * 128
    chunks = next((n for n in (6, 4, 3, 2) if hidden % (n * 128) == 0), 1)
    width = hidden // chunks
    rows = n_seq * CAP
    per = rows // n_head
    cfg = (n_seq, n_head, experts, chunks, width, heads, hd, half)
    square = (heads, hd, hd)
    vm = pltpu.VMEM
    dma = pltpu.SemaphoreType.DMA
    vmem, anywhere = pl.BlockSpec(memory_space=pltpu.VMEM), pl.BlockSpec(memory_space=pl.ANY)
    scratch = [
        vm((tokens, inner), BF16), vm((tokens, inner), BF16), vm((tokens, inner), BF16),
        vm((tokens, inner), BF16), vm((tokens, depth), BF16),
        vm((chunks, depth, width), BF16), vm((chunks, depth, width), BF16),
        vm((chunks, width, depth), BF16), vm((tokens, inner), BF16), vm((tokens, depth), BF16),
        vm((heads, tokens), F32), vm((tokens, heads), F32), vm((heads, hd), F32), vm((heads, hd), F32),
        vm(square, BF16), vm(square, BF16), vm(square, BF16), vm(square, BF16), vm(square, BF16),
        vm((tokens, inner), F32),
        vm((2 * experts * CAP, tokens), F32), vm((experts, 2 * CAP, half), BF16),
        vm((n_seq, 2 * CAP, half), BF16), vm((rows, depth), BF16),
        vm((chunks, n_head, 2, per, width), BF16), vm((chunks, n_head - 1, 2, per, width), BF16),
        vm((chunks, n_head, per, width), BF16), vm((rows, depth), F32),
        vm((n_seq, 2 * CAP, half), BF16), vm((n_seq, 2 * CAP, half), BF16),
        dma((5,)), dma((3, chunks)), dma((n_seq - 1,)), dma((n_seq - 1,)),
        dma((chunks, n_head - 1)), dma((chunks, n_head - 1)),
        dma((chunks, n_head - 1)), dma((chunks, n_head - 1)),
        dma((n_seq - 1,)), dma((n_seq - 1,)), dma((2, 4)), dma((2,)),
    ]
    results = pl.pallas_call(
        functools.partial(kernel, cfg),
        out_shape=(
            jax.ShapeDtypeStruct((tokens, inner), BF16),
            jax.ShapeDtypeStruct((tokens, depth), BF16),
        ),
        in_specs=[vmem] * 4 + [pl.BlockSpec(memory_space=pltpu.SMEM)] + [anywhere] * 8,
        out_specs=(anywhere, anywhere),
        scratch_shapes=scratch,
        compiler_params=pltpu.CompilerParams(
            collective_id=0, has_side_effects=True, vmem_limit_bytes=60 * 1024 * 1024
        ),
    )(
        log_decay, norm_gain.reshape(1, -1), expert_ids.T, route_weight.T, placement,
        queries, key_input, value_input, out_gate, features, gate_weight, up_weight, down_weight,
    )
    return pl.pallas_call(
        hand_over,
        out_shape=tuple(jax.ShapeDtypeStruct(a.shape, a.dtype) for a in results),
        in_specs=[anywhere] * 2,
        out_specs=(anywhere, anywhere),
        scratch_shapes=[dma((8,))],
        compiler_params=pltpu.CompilerParams(vmem_limit_bytes=60 * 1024 * 1024),
    )(*results)


def hand_over(a, b, a_out, b_out, sem):
    copies = []
    for src, dst in ((a, a_out), (b, b_out)):
        part = src.shape[0] // 4
        for i in range(4):
            rows = pl.ds(i * part, part)
            copies.append(pltpu.make_async_copy(src.at[rows], dst.at[rows], sem.at[len(copies)]))
    for copy in copies:
        copy.start()
    for copy in copies:
        copy.wait()


def solution(mesh):
    placed = (
        P("seq", "head"), P("seq", "head"), P("seq", "head"), P("seq", "head"),
        P("head", "seq"), P("head"), P("seq", "head"), P("seq", None), P("seq", None), P(),
        P("head", "seq"), P("head", "seq"), P("seq", "head"),
    )
    return jax.shard_map(
        per_device,
        mesh=mesh,
        in_specs=placed,
        out_specs=(P("seq", "head"), P("seq", "head")),
        check_vma=False,
    )
```

```python
import functools

import jax
import jax.numpy as jnp
from jax import lax
from jax.experimental import pallas as pl
from jax.experimental.pallas import tpu as pltpu
from jax.sharding import PartitionSpec as P

CAP = 8
norm_eps = 1e-06
SLOTS = 4
F32, BF16 = jnp.float32, jnp.bfloat16


def each(count, body):
    if count <= 8:
        for i in range(count):
            body(i)
    else:

        @pl.loop(0, count)
        def _(i):
            body(i)


def dot(a, b, ca=1, cb=0):
    return lax.dot_general(a, b, (((ca,), (cb,)), ((), ())), preferred_element_type=F32)


def kernel(
    cfg,
    ld, gain, ids, rw, place,
    q_hbm, k_hbm, v_hbm, g_hbm, f_hbm, wg_hbm, wu_hbm, wd_hbm,
    ao_hbm, mo_hbm,
    q, k, v, g, f, wg, wu, wd, ao, mo,
    cum, cum_t, carry, carry_in, loc, loc_in, s_in, s_out, st, intra,
    share, out_x, in_x, x, rs_out, rs_in, mid, hid, acc, out_y, in_y,
    local_sem, weight_sem, x_send, x_recv, rs_send, rs_recv, ag_send, ag_recv,
    y_send, y_recv, chain_sem, out_sem,
):
    n_seq, n_head, experts, chunks, width, heads, hd, half = cfg
    tokens = q.shape[0]
    depth = f.shape[1]
    group = n_seq // experts
    rows = n_seq * CAP
    per = rows // n_head
    seq, head = lax.axis_index("seq"), lax.axis_index("head")
    core, chip, chips = lax.rem(seq, 2), seq // 2, n_seq // 2

    def at_seq(i):
        return {"seq": i}

    def at_head(i):
        return {"head": i}

    barrier = pltpu.get_barrier_semaphore()

    def greet_seq(r):
        pl.semaphore_signal(barrier, inc=1, device_id=at_seq(lax.rem(seq + r + 1, n_seq)),
                            device_id_type=pl.DeviceIdType.MESH)

    def greet_head(r):
        pl.semaphore_signal(barrier, inc=1, device_id=at_head(lax.rem(head + r + 1, n_head)),
                            device_id_type=pl.DeviceIdType.MESH)

    each(n_seq - 1, greet_seq)
    each(n_head - 1, greet_head)

    local = [
        pltpu.make_async_copy(a, b, local_sem.at[i])
        for i, (a, b) in enumerate(((f_hbm, f), (k_hbm, k), (v_hbm, v), (q_hbm, q), (g_hbm, g)))
    ]
    for copy in local[:3]:
        copy.start()
    up_copies, down_copies = [], []
    for c in range(chunks):
        cols = pl.ds(c * width, width)
        up_copies.append((
            pltpu.make_async_copy(wg_hbm.at[:, cols], wg.at[c], weight_sem.at[0, c]),
            pltpu.make_async_copy(wu_hbm.at[:, cols], wu.at[c], weight_sem.at[1, c]),
        ))
        down_copies.append(pltpu.make_async_copy(wd_hbm.at[cols, :], wd.at[c], weight_sem.at[2, c]))
    for a, b in up_copies:
        a.start()
        b.start()
    for copy in local[3:]:
        copy.start()
    for copy in down_copies:
        copy.start()

    t_row = lax.broadcasted_iota(jnp.int32, (tokens, tokens), 0)
    t_col = lax.broadcasted_iota(jnp.int32, (tokens, tokens), 1)
    lower = (t_row >= t_col).astype(F32).astype(BF16)
    slots = experts * CAP
    slot = lax.broadcasted_iota(jnp.int32, (slots, tokens), 0)
    wanted = jnp.full((slots, tokens), -1, jnp.int32)
    for j in range(experts):
        wanted = jnp.where(slot // CAP == j, place[j], wanted)
    first = (ids[0:1] == wanted).astype(F32)
    second = (ids[1:2] == wanted).astype(F32)
    match = first + second
    rank = dot(match.astype(BF16), lower, 1, 1)
    hit = jnp.where(rank == (slot % CAP + 1).astype(F32), match, 0.0)
    weight = hit * (first * rw[0:1] + second * rw[1:2])
    weight_high = weight.astype(BF16)
    share[0:slots] = weight_high.astype(F32)
    share[slots:] = weight - weight_high.astype(F32)
    local[0].wait()
    picked = dot(hit.astype(BF16), f[...])
    pad = 2 * half - depth

    def pack(a):
        high = a[:, half:]
        if pad:
            high = jnp.concatenate([high, jnp.zeros((CAP, pad), F32)], axis=1)
        return jnp.concatenate([a[:, :half], high], axis=0).astype(BF16)

    for j in range(experts):
        out_x[j] = pack(picked[j * CAP:(j + 1) * CAP])
    in_x[seq] = out_x[seq // group]
    pl.semaphore_wait(barrier, n_seq - 1 + n_head - 1)

    def x_copy(r):
        to = lax.rem(seq + r + 1, n_seq)
        return pltpu.make_async_remote_copy(
            out_x.at[to // group], in_x.at[seq], x_send.at[r], x_recv.at[r],
            device_id=at_seq(to), device_id_type=pl.DeviceIdType.MESH)

    def x_arrival(r):
        src = lax.rem(seq + n_seq - r - 1, n_seq)
        return pltpu.make_async_remote_copy(
            out_x.at[0], in_x.at[src], x_send.at[r], x_recv.at[r],
            device_id=at_seq(src), device_id_type=pl.DeviceIdType.MESH)

    each(n_seq - 1, lambda r: x_copy(r).start())

    rest = ld[...]
    total, total_t = 0.0, 0.0
    for _ in range(3):
        piece = rest.astype(BF16)
        rest = rest - piece.astype(F32)
        total = total + dot(piece, lower, 1, 1)
        total_t = total_t + dot(lower, piece, 1, 1)
    cum[...] = total
    cum_t[...] = total_t
    carry[...] = jnp.broadcast_to(jnp.exp(total[:, tokens - 1:]), carry.shape)
    head_lane = lax.broadcasted_iota(jnp.int32, (tokens, heads), 1)

    def column(h):
        return jnp.sum(jnp.where(head_lane == h, cum_t[...], 0.0), axis=1, keepdims=True)

    def cols_of(h):
        return pl.ds(pl.multiple_of(h * hd, hd), hd)

    local[1].wait()
    local[2].wait()

    def own_state(h, _):
        col = column(h)
        scaled = k[:, cols_of(h)].astype(F32) * jnp.exp(col[tokens - 1:] - col)
        loc[h] = dot(scaled.astype(BF16), v[:, cols_of(h)], 0, 0).astype(BF16)
        return 0

    lax.fori_loop(0, heads, own_state, 0, unroll=True)

    def pair_copy(ref, to, n, other):
        return pltpu.make_async_remote_copy(
            ref, to, chain_sem.at[0, n], chain_sem.at[1, n],
            device_id=at_seq(other), device_id_type=pl.DeviceIdType.MESH)

    partner = seq + 1 - 2 * core
    onward = lax.rem(seq + 2, n_seq)
    loc_copy = pair_copy(loc, loc_in, 0, partner)
    carry_copy = pair_copy(carry, carry_in, 1, partner)
    state_copy = pair_copy(s_out, s_in, 2, onward)
    share_copy = pair_copy(s_in, st, 3, partner)

    @pl.when(core == 0)
    def _():
        loc_copy.start()
        carry_copy.start()

    def chain(which):
        @pl.when((core == 1) & which)
        def _():
            loc_copy.wait_recv()
            carry_copy.wait_recv()

            @pl.when(chip == 0)
            def _():
                s_in[...] = jnp.zeros_like(s_in)

            @pl.when(chip > 0)
            def _():
                state_copy.wait_recv()

            share_copy.start()

            def step(h, _):
                mid = carry_in[pl.ds(h, 1)] * s_in[h].astype(F32) + loc_in[h].astype(F32)
                st[h] = mid.astype(BF16)
                s_out[h] = (carry[pl.ds(h, 1)] * mid + loc[h].astype(F32)).astype(BF16)
                return 0

            lax.fori_loop(0, heads, step, 0)

            @pl.when(chip < chips - 1)
            def _():
                state_copy.start()

    each(n_seq - 1, lambda r: x_arrival(r).wait_recv())
    both = in_x[...].astype(F32)
    low = both[:, :CAP].reshape(rows, half)
    high = both[:, CAP:].reshape(rows, half)[:, :depth - half]
    x[...] = jnp.concatenate([low, high], axis=1).astype(BF16)

    def rs_copy(c, r):
        to = lax.rem(head + r + 1, n_head)
        return pltpu.make_async_remote_copy(
            rs_out.at[c, to], rs_in.at[c, r], rs_send.at[c, r], rs_recv.at[c, r],
            device_id=at_head(to), device_id_type=pl.DeviceIdType.MESH)

    def ag_copy(c, r, src):
        to = lax.rem(head + r + 1, n_head)
        return pltpu.make_async_remote_copy(
            hid.at[c, src], hid.at[c, src], ag_send.at[c, r], ag_recv.at[c, r],
            device_id=at_head(to), device_id_type=pl.DeviceIdType.MESH)

    square = n_head == 4
    row = head // 2
    near = (head + 1 - 2 * (head - 2 * row), head + 2 - 4 * row)
    far = n_head - 1 - head

    def send(src, dst, sems, c, i, to):
        return pltpu.make_async_remote_copy(
            src, dst, sems[0].at[c, i], sems[1].at[c, i],
            device_id=at_head(to), device_id_type=pl.DeviceIdType.MESH)

    def rs_step(c, i):
        one, two = near[c % 2], near[1 - c % 2]
        src = (rs_out.at[c, far], rs_out.at[c, one], mid.at[c])[i]
        return send(src, rs_in.at[c, i], (rs_send, rs_recv), c, i, two if i == 2 else one)

    def ag_step(c, i):
        block = near[c % 2] if i == 2 else head
        to = near[1 - c % 2] if i == 2 else near[i]
        return send(hid.at[c, block], hid.at[c, block], (ag_send, ag_recv), c, i, to)

    def ag_landed(c, i):
        block = far if i == 2 else near[i]
        return send(hid.at[c, block], hid.at[c, block], (ag_send, ag_recv), c, i, near[0])

    def reduce_start(c):
        if square:
            rs_step(c, 0).start()
            rs_step(c, 1).start()
        else:
            each(n_head - 1, lambda r: rs_copy(c, r).start())

    def reduce_middle(c):
        if square:
            rs_step(c, 0).wait_recv()
            mid[c] = (rs_out[c, near[1 - c % 2]].astype(F32) + rs_in[c, 0].astype(F32)).astype(BF16)
            rs_step(c, 2).start()

    def reduce_end(c):
        total = rs_out[c, head].astype(F32)
        if square:
            rs_step(c, 1).wait_recv()
            rs_step(c, 2).wait_recv()
            return total + rs_in[c, 1].astype(F32) + rs_in[c, 2].astype(F32)
        each(n_head - 1, lambda r: rs_copy(c, r).wait_recv())
        for r in range(n_head - 1):
            total += rs_in[c, r].astype(F32)
        return total

    def gather_start(c):
        if square:
            ag_step(c, 0).start()
            ag_step(c, 1).start()
        else:
            each(n_head - 1, lambda r: ag_copy(c, r, head).start())

    def gather_middle(c):
        if square:
            ag_landed(c, c % 2).wait_recv()
            ag_step(c, 2).start()

    def gather_end(c):
        if square:
            ag_landed(c, 1 - c % 2).wait_recv()
            ag_landed(c, 2).wait_recv()
        else:
            each(n_head - 1, lambda r: ag_copy(c, r, lax.rem(head + n_head - r - 1, n_head)).wait_recv())

    for c in range(chunks):
        for which, ref in enumerate((wg, wu)):
            up_copies[c][which].wait()
            part = dot(x[...], ref[c])
            rs_out[c, :, which] = part.astype(BF16).reshape(n_head, per, width)
        reduce_start(c)
        if c == 0:
            chain(chip == 0)
        if c >= 2:
            reduce_middle(c - 2)

    def within(h, _):
        qh, kh, vh = (a[:, cols_of(h)] for a in (q, k, v))
        spread = column(h) - cum[pl.ds(h, 1)]
        decay = jnp.exp(jnp.where(t_row >= t_col, spread, -jnp.inf))
        probs = (dot(qh, kh, 1, 1) * decay).astype(BF16)
        intra[:, cols_of(h)] = dot(probs, vh)
        return 0

    local[3].wait()
    parts = min(chunks, heads)
    bounds = [heads * i // parts for i in range(parts + 1)]
    for c in range(chunks):
        if c < parts:
            lax.fori_loop(bounds[c], bounds[c + 1], within, 0, unroll=True)
        if max(0, chunks - 2) + c < chunks:
            reduce_middle(max(0, chunks - 2) + c)
        both = reduce_end(c)
        gate, up = both[0], both[1]
        hid[c, head] = (gate / (1.0 + jnp.exp(-gate)) * up).astype(BF16)
        gather_start(c)
        if c >= 1:
            gather_middle(c - 1)
        if c == 0:
            chain(chip == 1)
        if c == chunks - 1:
            chain(chip == 2)

    for c in range(chunks):
        if c == 0:
            gather_middle(chunks - 1)
        gather_end(c)
        down_copies[c].wait()
        part = dot(hid[c].reshape(rows, width), wd[c])
        if c == 0:
            acc[...] = part
        else:
            acc[...] += part

    for b in range(n_seq):
        out_y[b] = pack(acc[b * CAP:(b + 1) * CAP, :])
    in_y[seq] = out_y[seq]

    def y_copy(r):
        to = lax.rem(seq + r + 1, n_seq)
        return pltpu.make_async_remote_copy(
            out_y.at[to], in_y.at[seq], y_send.at[r], y_recv.at[r],
            device_id=at_seq(to), device_id_type=pl.DeviceIdType.MESH)

    def y_arrival(r):
        src = lax.rem(seq + n_seq - r - 1, n_seq)
        return pltpu.make_async_remote_copy(
            out_y.at[0], in_y.at[src], y_send.at[r], y_recv.at[r],
            device_id=at_seq(src), device_id_type=pl.DeviceIdType.MESH)

    each(n_seq - 1, lambda r: y_copy(r).start())
    chain(chip >= SLOTS - 1)

    @pl.when(core == 0)
    def _():
        share_copy.wait_recv()

    local[4].wait()

    def finish(h, _):
        cols = cols_of(h)
        mixed = intra[:, cols] + jnp.exp(column(h)) * dot(q[:, cols], st[h])
        power = jnp.mean(mixed * mixed, axis=-1, keepdims=True)
        gates = 1.0 / (1.0 + jnp.exp(-g[:, cols].astype(F32)))
        ao[:, cols] = (mixed * lax.rsqrt(power + norm_eps) * gain[:, cols] * gates).astype(BF16)
        return 0

    lax.fori_loop(0, heads, finish, 0, unroll=True)
    ao_copy = pltpu.make_async_copy(ao, ao_hbm, out_sem.at[0])
    ao_copy.start()

    each(n_seq - 1, lambda r: y_arrival(r).wait_recv())
    terms = []
    for i in range(group):
        outs = []
        for j in range(experts):
            both = in_y[j * group + i].astype(F32)
            outs.append(jnp.concatenate([both[:CAP], both[CAP:, :depth - half]], axis=1))
        terms += [jnp.concatenate(outs, axis=0).astype(BF16)] * 2
    weights = jnp.concatenate([share[...].astype(BF16)] * group, axis=0)
    mo[...] = dot(weights, jnp.concatenate(terms, axis=0), 0, 0).astype(BF16)
    mo_copy = pltpu.make_async_copy(mo, mo_hbm, out_sem.at[1])
    mo_copy.start()

    each(n_seq - 1, lambda r: x_copy(r).wait_send())
    each(n_seq - 1, lambda r: y_copy(r).wait_send())
    for c in range(chunks):
        if square:
            for i in range(n_head - 1):
                rs_step(c, i).wait_send()
                ag_step(c, i).wait_send()
        else:
            each(n_head - 1, lambda r, c=c: rs_copy(c, r).wait_send())
            each(n_head - 1, lambda r, c=c: ag_copy(c, r, head).wait_send())

    @pl.when(core == 0)
    def _():
        loc_copy.wait_send()
        carry_copy.wait_send()

    @pl.when(core == 1)
    def _():
        share_copy.wait_send()

        @pl.when(chip < chips - 1)
        def _():
            state_copy.wait_send()

    ao_copy.wait()
    mo_copy.wait()


def per_device(
    queries, key_input, value_input, out_gate, log_decay, norm_gain, features,
    expert_ids, route_weight, placement, gate_weight, up_weight, down_weight,
):
    n_seq, n_head = lax.axis_size("seq"), lax.axis_size("head")
    experts = placement.shape[0]
    tokens, inner = queries.shape
    heads = log_decay.shape[0]
    hd = inner // heads
    depth, hidden = gate_weight.shape
    half = -(-depth // 256) * 128
    chunks = next((n for n in (6, 4, 3, 2) if hidden % (n * 128) == 0), 1)
    width = hidden // chunks
    rows = n_seq * CAP
    per = rows // n_head
    cfg = (n_seq, n_head, experts, chunks, width, heads, hd, half)
    square = (heads, hd, hd)
    vm = pltpu.VMEM
    dma = pltpu.SemaphoreType.DMA
    vmem, anywhere = pl.BlockSpec(memory_space=pltpu.VMEM), pl.BlockSpec(memory_space=pl.ANY)
    scratch = [
        vm((tokens, inner), BF16), vm((tokens, inner), BF16), vm((tokens, inner), BF16),
        vm((tokens, inner), BF16), vm((tokens, depth), BF16),
        vm((chunks, depth, width), BF16), vm((chunks, depth, width), BF16),
        vm((chunks, width, depth), BF16), vm((tokens, inner), BF16), vm((tokens, depth), BF16),
        vm((heads, tokens), F32), vm((tokens, heads), F32), vm((heads, hd), F32), vm((heads, hd), F32),
        vm(square, BF16), vm(square, BF16), vm(square, BF16), vm(square, BF16), vm(square, BF16),
        vm((tokens, inner), F32),
        vm((2 * experts * CAP, tokens), F32), vm((experts, 2 * CAP, half), BF16),
        vm((n_seq, 2 * CAP, half), BF16), vm((rows, depth), BF16),
        vm((chunks, n_head, 2, per, width), BF16), vm((chunks, n_head - 1, 2, per, width), BF16),
        vm((chunks, 2, per, width), BF16),
        vm((chunks, n_head, per, width), BF16), vm((rows, depth), F32),
        vm((n_seq, 2 * CAP, half), BF16), vm((n_seq, 2 * CAP, half), BF16),
        dma((5,)), dma((3, chunks)), dma((n_seq - 1,)), dma((n_seq - 1,)),
        dma((chunks, n_head - 1)), dma((chunks, n_head - 1)),
        dma((chunks, n_head - 1)), dma((chunks, n_head - 1)),
        dma((n_seq - 1,)), dma((n_seq - 1,)), dma((2, 4)), dma((2,)),
    ]
    results = pl.pallas_call(
        functools.partial(kernel, cfg),
        out_shape=(
            jax.ShapeDtypeStruct((tokens, inner), BF16),
            jax.ShapeDtypeStruct((tokens, depth), BF16),
        ),
        in_specs=[vmem] * 4 + [pl.BlockSpec(memory_space=pltpu.SMEM)] + [anywhere] * 8,
        out_specs=(anywhere, anywhere),
        scratch_shapes=scratch,
        compiler_params=pltpu.CompilerParams(
            collective_id=0, has_side_effects=True, vmem_limit_bytes=60 * 1024 * 1024
        ),
    )(
        log_decay, norm_gain.reshape(1, -1), expert_ids.T, route_weight.T, placement,
        queries, key_input, value_input, out_gate, features, gate_weight, up_weight, down_weight,
    )
    return pl.pallas_call(
        hand_over,
        out_shape=tuple(jax.ShapeDtypeStruct(a.shape, a.dtype) for a in results),
        in_specs=[anywhere] * 2,
        out_specs=(anywhere, anywhere),
        scratch_shapes=[vm(a.shape, a.dtype) for a in results] + [dma((2, 4))],
        compiler_params=pltpu.CompilerParams(vmem_limit_bytes=60 * 1024 * 1024),
    )(*results)


def hand_over(a, b, a_out, b_out, a_held, b_held, sem):
    copies = []
    for src, held, dst in ((b, b_held, b_out), (a, a_held, a_out)):
        part = src.shape[0] // 2
        for i in range(2):
            rows = pl.ds(i * part, part)
            n = len(copies)
            copies.append((
                pltpu.make_async_copy(src.at[rows], held.at[rows], sem.at[0, n]),
                pltpu.make_async_copy(held.at[rows], dst.at[rows], sem.at[1, n]),
            ))
    for copy, _ in copies:
        copy.start()
    for copy, on in copies:
        copy.wait()
        on.start()
    for _, on in copies:
        on.wait()


def solution(mesh):
    placed = (
        P("seq", "head"), P("seq", "head"), P("seq", "head"), P("seq", "head"),
        P("head", "seq"), P("head"), P("seq", "head"), P("seq", None), P("seq", None), P(),
        P("head", "seq"), P("head", "seq"), P("seq", "head"),
    )
    return jax.shard_map(
        per_device,
        mesh=mesh,
        in_specs=placed,
        out_specs=(P("seq", "head"), P("seq", "head")),
        check_vma=False,
    )
```
